32 devices in a mesh: groups: 2 (over y), blk: 4 (over z), tgt: 4 (over x, core).
Axes of the slice: x: 2, y: 2, z: 4, core: 2. Of those that a mesh axis runs over, the one named last changes fastest.
Arguments:
- positions: float32 [3, 9984], P(None, ('groups', 'blk', 'tgt')), parts along dimension 1
- forces: float32 [3, 9984], P(None, ('groups', 'blk', 'tgt')), parts along dimension 1, may hold values from -8 to 8
- owner_map: int32 [32], P('groups'), parts along dimension 0, may hold values from 0 to 15, as said below
- near_target: int32 [4096], P(('groups', 'blk', 'tgt')), parts along dimension 0, may hold values from 0 to 15, as said below
- near_source: int32 [4096], P(('groups', 'blk', 'tgt')), parts along dimension 0, may hold values from 0 to 15, as said below
- near_patch: int32 [4096], P(('groups', 'blk', 'tgt')), parts along dimension 0, may hold values from 0 to 31
- patch_rows: int32 [32, 256], replicated, may hold values from 0 to 2663, as said below
- zone_rows: int32 [32, 128], replicated, may hold values from 0 to 311, as said below
Outputs:
- velocity: float32 [3, 9984], P(None, ('groups', 'blk', 'tgt')), parts along dimension 1
- patch_velocity: float32 [3, 9984], P(None, ('groups', 'blk', 'tgt')), parts along dimension 1
The draws below stay inside these ranges and needn't reach their ends.
There are 2 independent parts, one for each index of `groups`. The reference program is written for one: setup_inputs(seed, part) draws one part's arguments, and reference() takes and returns one part's arrays. A program takes and returns all parts, laid end to end along the dimension named above; an argument that names none is the same for every part. Nothing has to cross between parts.
Inputs may be any that keep to these rules, and one draw needn't show every extreme that they name: owner_map is a permutation; the vesicle in slot s is stored on the device of index s // 1 along blk+tgt. `near_source`: the 128 entries held by one device of blk+tgt name source vesicles stored on that device. `near_target`: among the 128 entries held by one device, at most 16 name target vesicles stored on any one device; one device, drawn anew, is named exactly 16 times by every device's entries. `patch_rows`: row p lists the nodes of a block of 16 x 16 cells of the 37 x 72 upsampled grid, node index = polar row * 72 + azimuthal column, azimuthal columns wrapping. `zone_rows`: row p lists the nodes of a block of 8 x 16 cells of the 13 x 24 coarse grid, node index = polar row * 24 + azimuthal column, azimuthal columns wrapping.
All inputs are finite; a program needn't handle non-finite values.
Results may differ from the reference program's by a relative error of at most 0.0003.
Values sent between devices are 32-bit elements; how exact they have to be, the bound alone decides.
A program may use at most 128 MiB of HBM per device.

```python
import math
import jax
import jax.numpy as jnp
import numpy as np
from jax import lax

THETA = 13
PHI = 24
FINE_THETA = 37
FINE_PHI = 72
PATCH_SIDE = 16
ZONE_POLAR = 8
ZONE_AROUND = 16
NPATCH = 32
VES_DEV = 1
PAIRS_DEV = 128
NODES = 312
FINE = 2664
PATCH = 256
ZONE = 128
VES = 16
PAIRS = 2048
CAP = 16


CELL_SPACING = 7.1


LONG_SEMI = 4.6


SHORT_SEMI = 2.6


BUMP_TOP = 0.02


AXIS_REACH = math.sqrt(LONG_SEMI * LONG_SEMI / 3.0 + 2.0 * SHORT_SEMI * SHORT_SEMI / 3.0)


def near_layout(key):
    device_count = VES // VES_DEV
    storage = jax.random.permutation(jax.random.fold_in(key, 101), VES).astype(jnp.int32)
    resident = jnp.zeros((VES,), jnp.int32).at[storage].set(jnp.arange(VES, dtype=jnp.int32))
    busiest = jax.random.randint(jax.random.fold_in(key, 102), (), 0, device_count)
    others = (jnp.arange(device_count * CAP - CAP, dtype=jnp.int32) // CAP + busiest + 1) % device_count

    def one_block(sender):
        block_key = jax.random.fold_in(key, sender + 1000)
        picked = jax.random.permutation(jax.random.fold_in(block_key, 1), others)[:PAIRS_DEV - CAP]
        owners = jnp.concatenate([jnp.full((CAP,), busiest, jnp.int32), picked.astype(jnp.int32)])
        owners = jax.random.permutation(jax.random.fold_in(block_key, 2), owners)
        target_slots = owners * VES_DEV + jax.random.randint(jax.random.fold_in(block_key, 3), (PAIRS_DEV,), 0, VES_DEV)
        source_slots = sender * VES_DEV + jax.random.randint(jax.random.fold_in(block_key, 4), (PAIRS_DEV,), 0, VES_DEV)
        return (resident[target_slots], resident[source_slots])
    target_ids, source_ids = jax.vmap(one_block)(jnp.arange(device_count, dtype=jnp.int32))
    return (storage, target_ids.reshape(PAIRS).astype(jnp.int32), source_ids.reshape(PAIRS).astype(jnp.int32))


def draw_owner_map(key, part):
    shared = near_layout(key)
    key = jax.random.fold_in(key, 11)
    return shared[0]


def draw_near_target(key, part):
    shared = near_layout(key)
    key = jax.random.fold_in(key, 12)
    return shared[1]


def draw_near_source(key, part):
    shared = near_layout(key)
    key = jax.random.fold_in(key, 13)
    return shared[2]


def draw_positions(key, part):
    key = jax.random.fold_in(key, 5)
    cell_key, jitter_key, scale_key, bump_key, axis_key = jax.random.split(key, 5)
    side_cells = min((count for count in range(1, VES + 1) if count ** 3 >= VES))
    cells = jax.random.permutation(cell_key, side_cells ** 3)[:VES].astype(jnp.int32)
    lattice = jnp.stack([cells // (side_cells * side_cells), cells // side_cells % side_cells, cells % side_cells]).astype(jnp.float32)
    signs = (2 * jax.random.randint(axis_key, (3, VES), 0, 2) - 1).astype(jnp.float32)
    sizes = jax.random.uniform(scale_key, (VES,), jnp.float32, 0.9, 1.0)
    long_axis = signs / math.sqrt(3.0)
    first_side = jnp.stack([signs[1], -signs[0], jnp.zeros((VES,), jnp.float32)]) / math.sqrt(2.0)
    second_side = jnp.cross(long_axis, first_side, axis=0)
    reach = 0.5 * CELL_SPACING - AXIS_REACH * (1.0 + BUMP_TOP) * sizes
    jitter = jax.random.uniform(jitter_key, (3, VES), jnp.float32, -0.95, 0.95) * reach[None, :]
    centers = (CELL_SPACING * lattice + jitter)[:, :, None]
    bumps = 1.0 + jax.random.uniform(bump_key, (1, VES, THETA * PHI), jnp.float32, -BUMP_TOP, BUMP_TOP)
    node_index = jnp.arange(THETA * PHI)
    polar_angle = ((node_index // PHI).astype(jnp.float32) + 0.5) * (jnp.pi / THETA)
    azimuth = (node_index % PHI).astype(jnp.float32) * (2.0 * jnp.pi / PHI)
    along = LONG_SEMI * jnp.cos(polar_angle)[None, None, :] * long_axis[:, :, None]
    across = SHORT_SEMI * jnp.sin(polar_angle)[None, None, :] * (jnp.cos(azimuth)[None, None, :] * first_side[:, :, None] + jnp.sin(azimuth)[None, None, :] * second_side[:, :, None])
    points = centers + sizes[None, :, None] * bumps * (along + across)
    return points.reshape(3, VES * THETA * PHI).astype(jnp.float32)


def draw_patch_rows(key, part):
    key = jax.random.fold_in(key, 7)
    row_key, column_key, shuffle_key = jax.random.split(key, 3)
    starts_polar = jax.random.randint(row_key, (NPATCH,), 0, FINE_THETA - PATCH_SIDE + 1)
    starts_around = jax.random.randint(column_key, (NPATCH,), 0, FINE_PHI)
    shuffled = jax.random.permutation(shuffle_key, NPATCH)
    starts_polar = starts_polar.at[shuffled[0]].set(FINE_THETA - PATCH_SIDE).at[shuffled[1]].set(0)
    starts_around = starts_around.at[shuffled[0]].set(FINE_PHI - PATCH_SIDE).at[shuffled[1]].set(0)
    within = jnp.arange(PATCH, dtype=jnp.int32)
    polar_rows = starts_polar[:, None] + within[None, :] // PATCH_SIDE
    around_columns = (starts_around[:, None] + within[None, :] % PATCH_SIDE) % FINE_PHI
    return (polar_rows * FINE_PHI + around_columns).astype(jnp.int32)


def draw_zone_rows(key, part):
    key = jax.random.fold_in(key, 8)
    row_key, column_key, shuffle_key = jax.random.split(key, 3)
    starts_polar = jax.random.randint(row_key, (NPATCH,), 0, THETA - ZONE_POLAR + 1)
    starts_around = jax.random.randint(column_key, (NPATCH,), 0, PHI)
    shuffled = jax.random.permutation(shuffle_key, NPATCH)
    starts_polar = starts_polar.at[shuffled[0]].set(THETA - ZONE_POLAR).at[shuffled[1]].set(0)
    starts_around = starts_around.at[shuffled[0]].set(PHI - ZONE_AROUND).at[shuffled[1]].set(0)
    within = jnp.arange(ZONE, dtype=jnp.int32)
    polar_rows = starts_polar[:, None] + within[None, :] // ZONE_AROUND
    around_columns = (starts_around[:, None] + within[None, :] % ZONE_AROUND) % PHI
    return (polar_rows * PHI + around_columns).astype(jnp.int32)


def with_ends(drawn, key, smallest, largest):
    place = [jax.random.randint(jax.random.fold_in(key, axis), (), 0, length) for axis, length in enumerate(drawn.shape)]
    longest = drawn.shape.index(max(drawn.shape))
    beside = place[:longest] + [(place[longest] + 1) % drawn.shape[longest]] + place[longest + 1:]
    return drawn.at[tuple(place)].set(smallest).at[tuple(beside)].set(largest)


def shard_levels(rng, extent, cuts, smallest, high):
    loudness, own = 1.0, jax.random.fold_in(rng, 6)
    for position, shards_of in cuts:
        steps = jnp.exp(jax.random.uniform(jax.random.fold_in(own, position), (shards_of,), jnp.float32, smallest / len(cuts), high / len(cuts)))
        loudness = loudness * jnp.repeat(steps, extent[position] // shards_of).reshape([-1 if axis == position else 1 for axis in range(len(extent))])
    return loudness


def gaussian(rng, shape, scale, limit, shards=(), held_as=jnp.bfloat16):
    gain = shard_levels(rng, shape, shards, -0.22, 0.18) if shards else 1.0
    result = jax.random.normal(rng, shape, jnp.float32) * scale * gain
    return jnp.minimum(jnp.maximum(result, -limit), limit).astype(held_as)


def setup_inputs(seed: int = 0, part: int = 0) -> dict:
    arg_keys = jax.random.split(jax.random.key(seed), 9)
    own_keys = jax.random.split(jax.random.fold_in(arg_keys[8], part), 9)
    return {
        "positions": draw_positions(jax.random.fold_in(jax.random.fold_in(arg_keys[8], part), 71), part),
        "forces": gaussian(own_keys[1], (3, VES * NODES), 1.5, 8.0, ((1, 16),), jnp.float32),
        "owner_map": draw_owner_map(jax.random.fold_in(jax.random.fold_in(arg_keys[8], part), 71), part),
        "near_target": draw_near_target(jax.random.fold_in(jax.random.fold_in(arg_keys[8], part), 71), part),
        "near_source": draw_near_source(jax.random.fold_in(jax.random.fold_in(arg_keys[8], part), 71), part),
        "near_patch": with_ends(jax.random.randint(own_keys[5], (PAIRS,), 0, NPATCH), jax.random.fold_in(own_keys[5], 1), 0, NPATCH - 1).astype(jnp.int32),
        "patch_rows": draw_patch_rows(jax.random.fold_in(arg_keys[8], 71), part),
        "zone_rows": draw_zone_rows(jax.random.fold_in(arg_keys[8], 71), part),
    }


FAR_BLOB = 0.09
NEAR_BLOB = 0.0025
STOKES_FACTOR = 1.0 / (8.0 * math.pi)

def polar_weights(coarse, fine_count):
    weights = np.zeros((fine_count, coarse), np.float32)
    for fine_row in range(fine_count):
        numerator = (2 * fine_row + 1) * coarse - fine_count
        denominator = 2 * fine_count
        lower_node = min(max(numerator // denominator, 0), coarse - 2)
        fraction = min(max((numerator - lower_node * denominator) / denominator, 0.0), 1.0)
        weights[fine_row, lower_node] += 1.0 - fraction
        weights[fine_row, lower_node + 1] += fraction
    return weights

def azimuth_weights(coarse, fine_count):
    weights = np.zeros((fine_count, coarse), np.float32)
    for fine_column in range(fine_count):
        numerator = fine_column * coarse
        lower_node = numerator // fine_count
        fraction = (numerator - lower_node * fine_count) / fine_count
        weights[fine_column, lower_node] += 1.0 - fraction
        weights[fine_column, (lower_node + 1) % coarse] += fraction
    return weights

def upsample(values):
    leading = values.shape[:-1]
    grid_values = values.reshape(leading + (THETA, PHI))
    polar_table = jnp.asarray(polar_weights(THETA, FINE_THETA), dtype=values.dtype)
    azimuth_table = jnp.asarray(azimuth_weights(PHI, FINE_PHI), dtype=values.dtype)
    refined = jnp.einsum('ia,rvab,jb->rvij', polar_table, grid_values, azimuth_table, precision=lax.Precision.HIGHEST)
    return refined.reshape(leading + (FINE_THETA * FINE_PHI,))

def blob_velocity(targets, sources, forcing, blob_size):
    deltas = targets[:, :, None] - sources[:, None, :]
    squared = lax.optimization_barrier(jnp.sum(deltas * deltas, axis=0))
    inverse = lax.rsqrt(squared + blob_size)
    inverse_cube = inverse * inverse * inverse
    projected = lax.optimization_barrier(jnp.sum(deltas * forcing[:, None, :], axis=0))
    direct = lax.optimization_barrier(jnp.sum(((squared + 2.0 * blob_size) * inverse_cube)[None] * forcing[:, None, :], axis=2))
    outer_term = lax.optimization_barrier(jnp.sum((projected * inverse_cube)[None] * deltas, axis=2))
    return STOKES_FACTOR * (direct + outer_term)

def reference(positions, forces, owner_map, near_target, near_source, near_patch, patch_rows, zone_rows):
    by_vesicle = positions.reshape(3, VES, NODES).transpose(1, 0, 2)

    def far_field(targets):
        return blob_velocity(targets, positions, forces, FAR_BLOB)
    velocity = lax.map(far_field, by_vesicle).transpose(1, 0, 2).reshape(3, VES * NODES)
    stacked = jnp.concatenate([positions, forces], axis=0).reshape(6, VES, NODES)
    refined = upsample(stacked)
    refined = jnp.concatenate([refined[:3], refined[3:] * (NODES / FINE)], axis=0)
    flat_fine = refined.reshape(6, VES * FINE)
    target_slot = owner_map[near_target].astype(jnp.int32)
    source_slot = owner_map[near_source].astype(jnp.int32)

    def add_pair(accumulated, record):
        target_index, source_index, patch_index = record
        fine_columns = (source_index * FINE + patch_rows[patch_index]).astype(jnp.int32)
        patch_values = jnp.take(flat_fine, fine_columns, axis=1)
        node_columns = (target_index * NODES + zone_rows[patch_index]).astype(jnp.int32)
        targets = jnp.take(positions, node_columns, axis=1)
        update = blob_velocity(targets, patch_values[:3], patch_values[3:], NEAR_BLOB)
        return (accumulated.at[:, node_columns].add(update), None)
    patch_velocity, unused = lax.scan(add_pair, jnp.zeros((3, VES * NODES), jnp.float32), (target_slot, source_slot, near_patch))
    return (velocity, patch_velocity)
```

```python
import functools
import math

import jax
import jax.numpy as jnp
import numpy as np
from jax import lax
from jax.experimental import pallas as pl
from jax.experimental.pallas import tpu as pltpu
from jax.sharding import PartitionSpec as P

THETA = 13
PHI = 24
FINE_THETA = 37
FINE_PHI = 72
NODES = 312
FINE = 2664
LANES = 128
WIDE = 384
SIDE = 16
ROW = FINE_PHI + SIDE

FAR_BLOB = 0.09
NEAR_BLOB = 0.0025
STOKES_FACTOR = 1.0 / (8.0 * math.pi)


def polar_taps():
    taps = []
    for fine_row in range(FINE_THETA):
        numerator = (2 * fine_row + 1) * THETA - FINE_THETA
        denominator = 2 * FINE_THETA
        lower_node = min(max(numerator // denominator, 0), THETA - 2)
        fraction = min(max((numerator - lower_node * denominator) / denominator, 0.0), 1.0)
        taps.append((lower_node, np.float32(1.0 - fraction), np.float32(fraction)))
    return taps


def pair_terms(x, y, f, blob, sums):
    d = [x[k] - y[k] for k in range(3)]
    squared = d[0] * d[0] + d[1] * d[1] + d[2] * d[2] + blob
    inverse = lax.rsqrt(squared)
    cube = inverse * inverse * inverse
    direct = inverse + blob * cube
    outer = (d[0] * f[0] + d[1] * f[1] + d[2] * f[2]) * cube
    return [sums[k] + (direct * f[k] + outer * d[k]) for k in range(3)]


def split3(value):
    high = value.astype(jnp.bfloat16)
    rest = value - high.astype(jnp.float32)
    middle = rest.astype(jnp.bfloat16)
    low = (rest - middle.astype(jnp.float32)).astype(jnp.bfloat16)
    return jnp.concatenate([high, middle, low], axis=0)


def one_hot(zone_row):
    nodes = lax.broadcasted_iota(jnp.int32, (WIDE, LANES), 0)
    return jnp.where(nodes == zone_row, 1.0, 0.0).astype(jnp.bfloat16)


def upsample(column, coarse, fine):
    for k in range(6):
        coarse[k] = jnp.broadcast_to(column[:, k : k + 1], (WIDE, LANES))
    taps = polar_taps()

    def one_component(k, carry):
        for row, (lower, low_weight, high_weight) in enumerate(taps):
            here = coarse[k, pl.ds(lower * PHI, PHI), :] * low_weight
            here = here + coarse[k, pl.ds((lower + 1) * PHI, PHI), :] * high_weight
            after = jnp.concatenate([here[1:], here[:1]], axis=0)
            third = np.float32(1.0 / 3.0)
            step = (after - here) * third
            fine[k, pl.ds(row * ROW, PHI, stride=3), :] = here
            fine[k, pl.ds(row * ROW + 1, PHI, stride=3), :] = here + step
            fine[k, pl.ds(row * ROW + 2, PHI, stride=3), :] = after - step
            fine[k, pl.ds(row * ROW + FINE_PHI, SIDE), :] = fine[k, pl.ds(row * ROW, SIDE), :]
        return carry

    lax.fori_loop(0, 6, one_component, 0)


def near_part(entries, patches, devices, target_ref, owner_ref, patch_ref, start_ref, zone_ref,
              blocks, fine, table, landed, partial):
    spots = jnp.concatenate([blocks[:, k, :] for k in range(3)], axis=0)
    spots = split3(spots)
    count = 3 * devices

    def gather_zone(p, carry):
        picked = jnp.dot(
            spots, one_hot(zone_ref[pl.ds(p, 1), :]), preferred_element_type=jnp.float32
        )
        table[p] = (picked[2 * count :] + picked[count : 2 * count]) + picked[:count]
        landed[p] = jnp.zeros((count, LANES), jnp.float32)
        return carry

    lax.fori_loop(0, patches, gather_zone, 0)

    def one_entry(e, carry):
        target = owner_ref[target_ref[e]]
        p = patch_ref[e]
        base = start_ref[p]
        x = [
            jnp.broadcast_to(table[p, pl.ds(k * devices + target, 1), :], (8, LANES))
            for k in range(3)
        ]
        sums = [jnp.zeros((8, LANES), jnp.float32)] * 3
        for row in range(SIDE):
            for half in range(2):
                at = pl.ds(base + row * ROW + half * 8, 8)
                y = [fine[k, at, :] for k in range(3)]
                f = [fine[k + 3, at, :] for k in range(3)]
                sums = pair_terms(x, y, f, NEAR_BLOB, sums)
        for k in range(3):
            at = pl.ds(k * devices + target, 1)
            landed[p, at, :] = landed[p, at, :] + jnp.sum(sums[k], axis=0, keepdims=True)
        return carry

    lax.fori_loop(0, entries, one_entry, 0)

    def scatter_zone(p, total):
        hot = one_hot(zone_ref[pl.ds(p, 1), :])
        moved = lax.dot_general(
            split3(landed[p]), hot, (((1,), (1,)), ((), ())), preferred_element_type=jnp.float32
        )
        return total + ((moved[2 * count :] + moved[count : 2 * count]) + moved[:count])

    total = lax.fori_loop(0, patches, scatter_zone, jnp.zeros((count, WIDE), jnp.float32))
    total = total * np.float32(STOKES_FACTOR * NODES / FINE)
    for k in range(3):
        partial[k] = total[k * devices : (k + 1) * devices, :NODES]


def far_part(devices, blocks, coarse, tails, sums_ref, velocity):
    lane = lax.broadcasted_iota(jnp.int32, (8, LANES), 1)

    def merge(b, carry):
        first = blocks[2 * b, :, pl.ds(2 * LANES, LANES)]
        second = blocks[2 * b + 1, :, pl.ds(2 * LANES, LANES)]
        tails[b] = jnp.where(lane < 64, first, pltpu.roll(second, 64, 1))
        return carry

    lax.fori_loop(0, devices // 2, merge, 0)
    group = 3

    def targets(g, carry):
        starts = [pl.multiple_of(g * (8 * group) + 8 * i, 8) for i in range(group)]
        x = [[coarse[k, pl.ds(s, 8), :] for k in range(3)] for s in starts]

        def sources(b, flat):
            sums = [list(flat[3 * i : 3 * i + 3]) for i in range(group)]
            rows = [
                lambda k, i=i, j=j: blocks[2 * b + i, pl.ds(k, 1), pl.ds(j * LANES, LANES)]
                for i in range(2)
                for j in range(2)
            ] + [lambda k: tails[b, pl.ds(k, 1), :]]
            for read in rows:
                values = [jnp.broadcast_to(read(k), (8, LANES)) for k in range(6)]
                for i in range(group):
                    sums[i] = pair_terms(x[i], values[:3], values[3:], FAR_BLOB, sums[i])
            return tuple(v for s in sums for v in s)

        flat = tuple(jnp.zeros((8, LANES), jnp.float32) for _ in range(3 * group))
        flat = lax.fori_loop(0, devices // 2, sources, flat)
        for i in range(group):
            for k in range(3):
                sums_ref[k, pl.ds(starts[i], 8), :] = flat[3 * i + k]
        return carry

    lax.fori_loop(0, NODES // (8 * group), targets, 0)
    ones = jnp.ones((8, LANES), jnp.float32)
    for k in range(3):
        total = lax.dot_general(
            ones, sums_ref[k], (((1,), (1,)), ((), ())),
            precision=lax.Precision.HIGHEST, preferred_element_type=jnp.float32,
        )
        velocity[k : k + 1, :] = total[:1] * np.float32(STOKES_FACTOR)


def interactions(entries, patches, devices, target_ref, owner_ref, patch_ref, start_ref, zone_ref,
                 own_ref, blocks, velocity, partial, coarse, fine, table, landed, tails, sums_ref):
    upsample(own_ref[...].T, coarse, fine)
    near_part(entries, patches, devices, target_ref, owner_ref, patch_ref, start_ref, zone_ref,
              blocks, fine, table, landed, partial)
    far_part(devices, blocks, coarse, tails, sums_ref, velocity)


def patch_starts(patch_rows):
    polar = jnp.min(patch_rows // FINE_PHI, axis=1)
    around = patch_rows % FINE_PHI
    lowest = jnp.min(around, axis=1)
    wrapped = jnp.max(around, axis=1) - lowest >= SIDE
    late = jnp.min(jnp.where(around >= FINE_PHI // 2, around, FINE_PHI), axis=1)
    return polar * ROW + jnp.where(wrapped, late, lowest)


def on_device(
    positions, forces, owner_map, near_target, near_source, near_patch, patch_rows, zone_rows
):
    devices = lax.axis_size(("blk", "tgt"))
    entries = near_target.shape[0]
    patches = patch_rows.shape[0]
    own = jnp.pad(jnp.concatenate([positions, forces], axis=0), ((0, 2), (0, WIDE - NODES)))
    blocks = lax.all_gather(own, ("blk", "tgt"), axis=0)
    smem = pl.BlockSpec(memory_space=pltpu.SMEM)
    vmem = pl.BlockSpec(memory_space=pltpu.VMEM)
    velocity, partial = pl.pallas_call(
        functools.partial(interactions, entries, patches, devices),
        out_shape=(
            jax.ShapeDtypeStruct((3, NODES), jnp.float32),
            jax.ShapeDtypeStruct((3, devices, NODES), jnp.float32),
        ),
        in_specs=[smem] * 4 + [vmem] * 3,
        out_specs=(vmem, vmem),
        scratch_shapes=[
            pltpu.VMEM((6, WIDE, LANES), jnp.float32),
            pltpu.VMEM((6, FINE_THETA * ROW, LANES), jnp.float32),
            pltpu.VMEM((patches, 3 * devices, LANES), jnp.float32),
            pltpu.VMEM((patches, 3 * devices, LANES), jnp.float32),
            pltpu.VMEM((devices // 2, 8, LANES), jnp.float32),
            pltpu.VMEM((3, NODES, LANES), jnp.float32),
        ],
        compiler_params=pltpu.CompilerParams(vmem_limit_bytes=50 * 1024 * 1024),
    )(near_target, owner_map, near_patch, patch_starts(patch_rows), zone_rows, own, blocks)
    patch_velocity = lax.psum_scatter(partial, ("blk", "tgt"), scatter_dimension=1, tiled=True)
    return velocity, patch_velocity.reshape(3, NODES)


def solution(mesh):
    nodes = P(None, ("groups", "blk", "tgt"))
    pairs = P(("groups", "blk", "tgt"))
    in_specs = (nodes, nodes, P("groups"), pairs, pairs, pairs, P(), P())
    return jax.shard_map(
        on_device, mesh=mesh, in_specs=in_specs, out_specs=(nodes, nodes), check_vma=False
    )
```

```python
import functools
import math

import jax
import jax.numpy as jnp
import numpy as np
from jax import lax
from jax.experimental import pallas as pl
from jax.experimental.pallas import tpu as pltpu
from jax.sharding import PartitionSpec as P

THETA = 13
PHI = 24
FINE_THETA = 37
FINE_PHI = 72
NODES = 312
FINE = 2664
LANES = 128
WIDE = 384
SIDE = 16
ROW = FINE_PHI + SIDE

FAR_BLOB = 0.09
NEAR_BLOB = 0.0025
STOKES_FACTOR = 1.0 / (8.0 * math.pi)
MESH = pl.DeviceIdType.MESH


def polar_taps():
    taps = []
    for fine_row in range(FINE_THETA):
        numerator = (2 * fine_row + 1) * THETA - FINE_THETA
        denominator = 2 * FINE_THETA
        lower_node = min(max(numerator // denominator, 0), THETA - 2)
        fraction = min(max((numerator - lower_node * denominator) / denominator, 0.0), 1.0)
        taps.append((lower_node, np.float32(1.0 - fraction), np.float32(fraction)))
    return taps


def pair_terms(x, y, f, blob, sums):
    d = [x[k] - y[k] for k in range(3)]
    squared = d[0] * d[0] + d[1] * d[1] + d[2] * d[2] + blob
    inverse = lax.rsqrt(squared)
    cube = inverse * inverse * inverse
    direct = inverse + blob * cube
    outer = (d[0] * f[0] + d[1] * f[1] + d[2] * f[2]) * cube
    return [sums[k] + (direct * f[k] + outer * d[k]) for k in range(3)]


def split3(value):
    high = value.astype(jnp.bfloat16)
    rest = value - high.astype(jnp.float32)
    middle = rest.astype(jnp.bfloat16)
    low = (rest - middle.astype(jnp.float32)).astype(jnp.bfloat16)
    return jnp.concatenate([high, middle, low], axis=0)


def one_hot(zone_row):
    nodes = lax.broadcasted_iota(jnp.int32, (WIDE, LANES), 0)
    return jnp.where(nodes == zone_row, 1.0, 0.0).astype(jnp.bfloat16)


def upsample(column, coarse, fine):
    for k in range(6):
        coarse[k] = jnp.broadcast_to(column[:, k : k + 1], (WIDE, LANES))
    taps = polar_taps()

    def one_component(k, carry):
        for row, (lower, low_weight, high_weight) in enumerate(taps):
            here = coarse[k, pl.ds(lower * PHI, PHI), :] * low_weight
            here = here + coarse[k, pl.ds((lower + 1) * PHI, PHI), :] * high_weight
            after = jnp.concatenate([here[1:], here[:1]], axis=0)
            third = np.float32(1.0 / 3.0)
            step = (after - here) * third
            fine[k, pl.ds(row * ROW, PHI, stride=3), :] = here
            fine[k, pl.ds(row * ROW + 1, PHI, stride=3), :] = here + step
            fine[k, pl.ds(row * ROW + 2, PHI, stride=3), :] = after - step
            fine[k, pl.ds(row * ROW + FINE_PHI, SIDE), :] = fine[k, pl.ds(row * ROW, SIDE), :]
        return carry

    lax.fori_loop(0, 6, one_component, 0)


def near_part(entries, patches, devices, target_ref, owner_ref, patch_ref, start_ref, zone_ref,
              blocks, fine, table, landed, partial):
    spots = jnp.concatenate([blocks[:, k, :] for k in range(3)], axis=0)
    spots = split3(spots)
    count = 3 * devices

    def gather_zone(p, carry):
        picked = jnp.dot(
            spots, one_hot(zone_ref[pl.ds(p, 1), :]), preferred_element_type=jnp.float32
        )
        table[p] = (picked[2 * count :] + picked[count : 2 * count]) + picked[:count]
        landed[p] = jnp.zeros((count, LANES), jnp.float32)
        return carry

    lax.fori_loop(0, patches, gather_zone, 0)

    def one_entry(e, carry):
        target = owner_ref[target_ref[e]]
        p = patch_ref[e]
        base = start_ref[p]
        x = [
            jnp.broadcast_to(table[p, pl.ds(k * devices + target, 1), :], (8, LANES))
            for k in range(3)
        ]
        sums = [jnp.zeros((8, LANES), jnp.float32)] * 3
        for row in range(SIDE):
            for half in range(2):
                at = pl.ds(base + row * ROW + half * 8, 8)
                y = [fine[k, at, :] for k in range(3)]
                f = [fine[k + 3, at, :] for k in range(3)]
                sums = pair_terms(x, y, f, NEAR_BLOB, sums)
        for k in range(3):
            at = pl.ds(k * devices + target, 1)
            landed[p, at, :] = landed[p, at, :] + jnp.sum(sums[k], axis=0, keepdims=True)
        return carry

    lax.fori_loop(0, entries, one_entry, 0)

    def scatter_zone(p, total):
        hot = one_hot(zone_ref[pl.ds(p, 1), :])
        moved = lax.dot_general(
            split3(landed[p]), hot, (((1,), (1,)), ((), ())), preferred_element_type=jnp.float32
        )
        return total + ((moved[2 * count :] + moved[count : 2 * count]) + moved[:count])

    total = lax.fori_loop(0, patches, scatter_zone, jnp.zeros((count, WIDE), jnp.float32))
    total = total * np.float32(STOKES_FACTOR * NODES / FINE)
    for k in range(3):
        partial[:, k, :] = total[k * devices : (k + 1) * devices]


def far_part(devices, blocks, coarse, tails, sums_ref, velocity):
    lane = lax.broadcasted_iota(jnp.int32, (8, LANES), 1)

    def merge(b, carry):
        first = blocks[2 * b, :, pl.ds(2 * LANES, LANES)]
        second = blocks[2 * b + 1, :, pl.ds(2 * LANES, LANES)]
        tails[b] = jnp.where(lane < 64, first, pltpu.roll(second, 64, 1))
        return carry

    lax.fori_loop(0, devices // 2, merge, 0)
    group = 3

    def targets(g, carry):
        starts = [pl.multiple_of(g * (8 * group) + 8 * i, 8) for i in range(group)]
        x = [[coarse[k, pl.ds(s, 8), :] for k in range(3)] for s in starts]

        def sources(b, flat):
            sums = [list(flat[3 * i : 3 * i + 3]) for i in range(group)]
            rows = [
                lambda k, i=i, j=j: blocks[2 * b + i, pl.ds(k, 1), pl.ds(j * LANES, LANES)]
                for i in range(2)
                for j in range(2)
            ] + [lambda k: tails[b, pl.ds(k, 1), :]]
            for read in rows:
                values = [jnp.broadcast_to(read(k), (8, LANES)) for k in range(6)]
                for i in range(group):
                    sums[i] = pair_terms(x[i], values[:3], values[3:], FAR_BLOB, sums[i])
            return tuple(v for s in sums for v in s)

        flat = tuple(jnp.zeros((8, LANES), jnp.float32) for _ in range(3 * group))
        flat = lax.fori_loop(0, devices // 2, sources, flat)
        for i in range(group):
            for k in range(3):
                sums_ref[k, pl.ds(starts[i], 8), :] = flat[3 * i + k]
        return carry

    lax.fori_loop(0, NODES // (8 * group), targets, 0)
    ones = jnp.ones((8, LANES), jnp.float32)
    for k in range(3):
        total = lax.dot_general(
            ones, sums_ref[k], (((1,), (1,)), ((), ())),
            precision=lax.Precision.HIGHEST, preferred_element_type=jnp.float32,
        )
        velocity[k : k + 1, :] = total[:1] * np.float32(STOKES_FACTOR)


def near_kernel(entries, patches, devices, target_ref, owner_ref, patch_ref, start_ref, zone_ref,
                own_ref, blocks, partial, coarse, fine, table, landed):
    upsample(own_ref[...].T, coarse, fine)
    near_part(entries, patches, devices, target_ref, owner_ref, patch_ref, start_ref, zone_ref,
              blocks, fine, table, landed, partial)


def greet(me, devices, inner):
    barrier = pltpu.get_barrier_semaphore()

    def signal(i, carry):
        pl.semaphore_signal(
            barrier, inc=1, device_id=address(me, i, devices, inner), device_id_type=MESH
        )
        return carry

    lax.fori_loop(1, devices, signal, 0)
    pl.semaphore_wait(barrier, devices - 1)


def address(me, step, devices, inner):
    peer = lax.rem(me + step, devices)
    return {"blk": peer // inner, "tgt": lax.rem(peer, inner)}


def gather_kernel(devices, inner, own_ref, blocks, send_sem, recv_sem):
    me = lax.axis_index("blk") * inner + lax.axis_index("tgt")

    def copy(step, slot):
        return pltpu.make_async_remote_copy(
            src_ref=own_ref, dst_ref=blocks.at[slot], send_sem=send_sem.at[step],
            recv_sem=recv_sem.at[slot], device_id=address(me, step, devices, inner),
            device_id_type=MESH,
        )

    greet(me, devices, inner)

    def start(step, carry):
        copy(step, me).start()
        return carry

    lax.fori_loop(1, devices, start, 0)
    blocks[me] = own_ref[...]

    def finish(step, carry):
        copy(step, lax.rem(me + devices - step, devices)).wait()
        return carry

    lax.fori_loop(1, devices, finish, 0)


def exchange_kernel(devices, inner, own_ref, blocks, partial, velocity, patch_velocity,
                    coarse, tails, sums_ref, landing, send_sem, recv_sem):
    me = lax.axis_index("blk") * inner + lax.axis_index("tgt")

    def copy(step, slot):
        return pltpu.make_async_remote_copy(
            src_ref=partial.at[lax.rem(me + step, devices)], dst_ref=landing.at[slot],
            send_sem=send_sem.at[step], recv_sem=recv_sem.at[slot],
            device_id=address(me, step, devices, inner), device_id_type=MESH,
        )

    greet(me, devices, inner)

    def start(step, carry):
        copy(step, me).start()
        return carry

    lax.fori_loop(1, devices, start, 0)
    column = own_ref[...].T
    for k in range(3):
        coarse[k] = jnp.broadcast_to(column[:, k : k + 1], (WIDE, LANES))
    far_part(devices, blocks, coarse, tails, sums_ref, velocity)

    def finish(step, total):
        slot = lax.rem(me + devices - step, devices)
        copy(step, slot).wait()
        return total + landing[slot]

    total = lax.fori_loop(1, devices, finish, partial[me])
    patch_velocity[...] = total[:3, :NODES]


def patch_starts(patch_rows):
    polar = jnp.min(patch_rows // FINE_PHI, axis=1)
    around = patch_rows % FINE_PHI
    lowest = jnp.min(around, axis=1)
    wrapped = jnp.max(around, axis=1) - lowest >= SIDE
    late = jnp.min(jnp.where(around >= FINE_PHI // 2, around, FINE_PHI), axis=1)
    return polar * ROW + jnp.where(wrapped, late, lowest)


def on_device(
    positions, forces, owner_map, near_target, near_source, near_patch, patch_rows, zone_rows
):
    devices = lax.axis_size(("blk", "tgt"))
    entries = near_target.shape[0]
    patches = patch_rows.shape[0]
    own = jnp.pad(jnp.concatenate([positions, forces], axis=0), ((0, 2), (0, WIDE - NODES)))
    inner = lax.axis_size("tgt")
    smem = pl.BlockSpec(memory_space=pltpu.SMEM)
    vmem = pl.BlockSpec(memory_space=pltpu.VMEM)
    block_shape = jax.ShapeDtypeStruct((devices, 8, WIDE), jnp.float32)
    node_shape = jax.ShapeDtypeStruct((3, NODES), jnp.float32)
    semaphores = [pltpu.SemaphoreType.DMA((devices,))] * 2
    blocks = pl.pallas_call(
        functools.partial(gather_kernel, devices, inner),
        out_shape=block_shape,
        in_specs=[vmem],
        out_specs=vmem,
        scratch_shapes=semaphores,
        compiler_params=pltpu.CompilerParams(collective_id=0, has_side_effects=True),
    )(own)
    partial = pl.pallas_call(
        functools.partial(near_kernel, entries, patches, devices),
        out_shape=block_shape,
        in_specs=[smem] * 4 + [vmem] * 3,
        out_specs=vmem,
        scratch_shapes=[
            pltpu.VMEM((6, WIDE, LANES), jnp.float32),
            pltpu.VMEM((6, FINE_THETA * ROW, LANES), jnp.float32),
            pltpu.VMEM((patches, 3 * devices, LANES), jnp.float32),
            pltpu.VMEM((patches, 3 * devices, LANES), jnp.float32),
        ],
        compiler_params=pltpu.CompilerParams(vmem_limit_bytes=50 * 1024 * 1024),
    )(near_target, owner_map, near_patch, patch_starts(patch_rows), zone_rows, own, blocks)
    return pl.pallas_call(
        functools.partial(exchange_kernel, devices, inner),
        out_shape=(node_shape, node_shape),
        in_specs=[vmem] * 3,
        out_specs=(vmem, vmem),
        scratch_shapes=[
            pltpu.VMEM((3, WIDE, LANES), jnp.float32),
            pltpu.VMEM((devices // 2, 8, LANES), jnp.float32),
            pltpu.VMEM((3, NODES, LANES), jnp.float32),
            pltpu.VMEM((devices, 8, WIDE), jnp.float32),
        ] + semaphores,
        compiler_params=pltpu.CompilerParams(
            collective_id=1, has_side_effects=True, vmem_limit_bytes=50 * 1024 * 1024
        ),
    )(own, blocks, partial)


def solution(mesh):
    nodes = P(None, ("groups", "blk", "tgt"))
    pairs = P(("groups", "blk", "tgt"))
    in_specs = (nodes, nodes, P("groups"), pairs, pairs, pairs, P(), P())
    return jax.shard_map(
        on_device, mesh=mesh, in_specs=in_specs, out_specs=(nodes, nodes), check_vma=False
    )
```

```python
import functools
import math

import jax
import jax.numpy as jnp
import numpy as np
from jax import lax
from jax.experimental import pallas as pl
from jax.experimental.pallas import tpu as pltpu
from jax.sharding import PartitionSpec as P

THETA = 13
PHI = 24
FINE_THETA = 37
FINE_PHI = 72
NODES = 312
FINE = 2664
LANES = 128
WIDE = 384
SIDE = 16
ROW = FINE_PHI + SIDE

FAR_BLOB = 0.09
NEAR_BLOB = 0.0025
STOKES_FACTOR = 1.0 / (8.0 * math.pi)
MESH = pl.DeviceIdType.MESH


def polar_taps():
    taps = []
    for fine_row in range(FINE_THETA):
        numerator = (2 * fine_row + 1) * THETA - FINE_THETA
        denominator = 2 * FINE_THETA
        lower_node = min(max(numerator // denominator, 0), THETA - 2)
        fraction = min(max((numerator - lower_node * denominator) / denominator, 0.0), 1.0)
        taps.append((lower_node, np.float32(1.0 - fraction), np.float32(fraction)))
    return taps


def pair_terms(x, y, f, blob, sums):
    d = [x[k] - y[k] for k in range(3)]
    squared = d[0] * d[0] + d[1] * d[1] + d[2] * d[2] + blob
    inverse = lax.rsqrt(squared)
    cube = inverse * inverse * inverse
    direct = inverse + blob * cube
    outer = (d[0] * f[0] + d[1] * f[1] + d[2] * f[2]) * cube
    return [sums[k] + (direct * f[k] + outer * d[k]) for k in range(3)]


def split3(value):
    high = value.astype(jnp.bfloat16)
    rest = value - high.astype(jnp.float32)
    middle = rest.astype(jnp.bfloat16)
    low = (rest - middle.astype(jnp.float32)).astype(jnp.bfloat16)
    return jnp.concatenate([high, middle, low], axis=0)


def zone_tables(patches, zone_ref, hot):
    nodes = lax.broadcasted_iota(jnp.int32, (WIDE, LANES), 0)
    for p in range(patches):
        found = nodes == zone_ref[p : p + 1, :]
        hot[:, p * LANES : (p + 1) * LANES] = jnp.where(found, 1.0, 0.0).astype(jnp.bfloat16)


def upsample(column, coarse, fine):
    for k in range(6):
        coarse[k] = jnp.broadcast_to(column[:, k : k + 1], (WIDE, LANES))
    taps = polar_taps()

    def one_component(k, carry):
        for row, (lower, low_weight, high_weight) in enumerate(taps):
            here = coarse[k, pl.ds(lower * PHI, PHI), :] * low_weight
            here = here + coarse[k, pl.ds((lower + 1) * PHI, PHI), :] * high_weight
            after = jnp.concatenate([here[1:], here[:1]], axis=0)
            third = np.float32(1.0 / 3.0)
            step = (after - here) * third
            fine[k, pl.ds(row * ROW, PHI, stride=3), :] = here
            fine[k, pl.ds(row * ROW + 1, PHI, stride=3), :] = here + step
            fine[k, pl.ds(row * ROW + 2, PHI, stride=3), :] = after - step
            fine[k, pl.ds(row * ROW + FINE_PHI, SIDE), :] = fine[k, pl.ds(row * ROW, SIDE), :]
        return carry

    lax.fori_loop(0, 6, one_component, 0)


def near_part(entries, patches, devices, target_ref, owner_ref, patch_ref, start_ref,
              listed_ref, blocks, fine, hot, table, results, partial):
    spots = jnp.concatenate([blocks[:, k, :] for k in range(3)], axis=0)
    spots = split3(spots)
    count = 3 * devices
    batch = 8

    for first in range(0, patches, batch):
        picked = jnp.dot(
            spots, hot[:, first * LANES : (first + batch) * LANES],
            preferred_element_type=jnp.float32,
        )
        picked = (picked[2 * count :] + picked[count : 2 * count]) + picked[:count]
        for i in range(batch):
            table[first + i] = picked[:, i * LANES : (i + 1) * LANES]

    def one_entry(e, carry):
        target = owner_ref[target_ref[e]]
        p = patch_ref[e]
        base = start_ref[p]
        x = [
            jnp.broadcast_to(table[p, pl.ds(k * devices + target, 1), :], (8, LANES))
            for k in range(3)
        ]
        sums = [jnp.zeros((8, LANES), jnp.float32)] * 3
        for row in range(SIDE):
            for half in range(2):
                at = pl.ds(base + row * ROW + half * 8, 8)
                y = [fine[k, at, :] for k in range(3)]
                f = [fine[k + 3, at, :] for k in range(3)]
                sums = pair_terms(x, y, f, NEAR_BLOB, sums)
        for k in range(3):
            results[k, pl.ds(e, 1), :] = jnp.sum(sums[k], axis=0, keepdims=True)
        return carry

    lax.fori_loop(0, entries, one_entry, 0)

    named = listed_ref[0:1, :]
    slot = lax.fori_loop(
        0, devices, lambda v, found: jnp.where(named == v, owner_ref[v], found),
        jnp.zeros((1, entries), jnp.int32),
    )
    slots = lax.broadcasted_iota(jnp.int32, (devices, entries), 0)
    here = slots == slot
    region = listed_ref[1:2, :]
    values = split3(jnp.concatenate([results[k] for k in range(3)], axis=1))
    total = [jnp.zeros((3 * devices, WIDE), jnp.float32) for _ in range(3)]
    for first in range(0, patches, batch):
        chosen = jnp.concatenate(
            [jnp.where(here & (region == first + i), 1.0, 0.0) for i in range(batch)], axis=0
        ).astype(jnp.bfloat16)
        landed = jnp.dot(
            jnp.concatenate([chosen] * 3, axis=1), values, preferred_element_type=jnp.float32
        )
        for k in range(3):
            mine = landed[:, k * LANES : (k + 1) * LANES]
            mine = jnp.concatenate(
                [mine[i * devices : (i + 1) * devices] for i in range(batch)], axis=1
            )
            total[k] = total[k] + lax.dot_general(
                split3(mine), hot[:, first * LANES : (first + batch) * LANES],
                (((1,), (1,)), ((), ())), preferred_element_type=jnp.float32,
            )
    for k in range(3):
        moved = (total[k][2 * devices :] + total[k][devices : 2 * devices]) + total[k][:devices]
        partial[:, k, :] = moved * np.float32(STOKES_FACTOR * NODES / FINE)


def far_part(devices, blocks, coarse, tails, sums_ref, velocity):
    lane = lax.broadcasted_iota(jnp.int32, (8, LANES), 1)

    def merge(b, carry):
        first = blocks[2 * b, :, pl.ds(2 * LANES, LANES)]
        second = blocks[2 * b + 1, :, pl.ds(2 * LANES, LANES)]
        tails[b] = jnp.where(lane < 64, first, pltpu.roll(second, 64, 1))
        return carry

    lax.fori_loop(0, devices // 2, merge, 0)
    group = 3

    def targets(g, carry):
        starts = [pl.multiple_of(g * (8 * group) + 8 * i, 8) for i in range(group)]
        x = [[coarse[k, pl.ds(s, 8), :] for k in range(3)] for s in starts]

        def sources(b, flat):
            sums = [list(flat[3 * i : 3 * i + 3]) for i in range(group)]
            rows = [
                lambda k, i=i, j=j: blocks[2 * b + i, pl.ds(k, 1), pl.ds(j * LANES, LANES)]
                for i in range(2)
                for j in range(2)
            ] + [lambda k: tails[b, pl.ds(k, 1), :]]
            for read in rows:
                values = [jnp.broadcast_to(read(k), (8, LANES)) for k in range(6)]
                for i in range(group):
                    sums[i] = pair_terms(x[i], values[:3], values[3:], FAR_BLOB, sums[i])
            return tuple(v for s in sums for v in s)

        flat = tuple(jnp.zeros((8, LANES), jnp.float32) for _ in range(3 * group))
        flat = lax.fori_loop(0, devices // 2, sources, flat)
        for i in range(group):
            for k in range(3):
                sums_ref[k, pl.ds(starts[i], 8), :] = flat[3 * i + k]
        return carry

    lax.fori_loop(0, NODES // (8 * group), targets, 0)
    ones = jnp.ones((8, LANES), jnp.float32)
    for k in range(3):
        total = lax.dot_general(
            ones, sums_ref[k], (((1,), (1,)), ((), ())),
            precision=lax.Precision.HIGHEST, preferred_element_type=jnp.float32,
        )
        velocity[k : k + 1, :] = total[:1] * np.float32(STOKES_FACTOR)


def greet(me, devices, inner):
    barrier = pltpu.get_barrier_semaphore()

    def signal(i, carry):
        pl.semaphore_signal(
            barrier, inc=1, device_id=address(me, i, devices, inner), device_id_type=MESH
        )
        return carry

    lax.fori_loop(1, devices, signal, 0)
    pl.semaphore_wait(barrier, devices - 1)


def address(me, step, devices, inner):
    peer = lax.rem(me + step, devices)
    return {"blk": peer // inner, "tgt": lax.rem(peer, inner)}


def interactions(entries, patches, devices, inner, target_ref, owner_ref, patch_ref, start_ref,
                 listed_ref, zone_ref, own_ref, velocity, patch_velocity, blocks, coarse, fine, hot,
                 table, results, partial, landing, tails, sums_ref, sent, arrived, returned, landed):
    me = lax.axis_index("blk") * inner + lax.axis_index("tgt")

    def spread(step, slot):
        return pltpu.make_async_remote_copy(
            src_ref=own_ref, dst_ref=blocks.at[slot], send_sem=sent.at[step],
            recv_sem=arrived.at[slot], device_id=address(me, step, devices, inner),
            device_id_type=MESH,
        )

    def give_back(step, slot):
        return pltpu.make_async_remote_copy(
            src_ref=partial.at[lax.rem(me + step, devices)], dst_ref=landing.at[slot],
            send_sem=returned.at[step], recv_sem=landed.at[slot],
            device_id=address(me, step, devices, inner), device_id_type=MESH,
        )

    greet(me, devices, inner)

    def start(step, carry):
        spread(step, me).start()
        return carry

    lax.fori_loop(1, devices, start, 0)
    blocks[me] = own_ref[...]
    upsample(own_ref[...].T, coarse, fine)
    zone_tables(patches, zone_ref, hot)

    def arrive(step, carry):
        spread(step, lax.rem(me + devices - step, devices)).wait()
        return carry

    lax.fori_loop(1, devices, arrive, 0)
    near_part(entries, patches, devices, target_ref, owner_ref, patch_ref, start_ref,
              listed_ref, blocks, fine, hot, table, results, partial)

    def start_back(step, carry):
        give_back(step, me).start()
        return carry

    lax.fori_loop(1, devices, start_back, 0)
    far_part(devices, blocks, coarse, tails, sums_ref, velocity)

    def finish(step, total):
        slot = lax.rem(me + devices - step, devices)
        give_back(step, slot).wait()
        return total + landing[slot]

    total = lax.fori_loop(1, devices, finish, partial[me])
    patch_velocity[...] = total[:3, :NODES]


def patch_starts(patch_rows):
    polar = jnp.min(patch_rows // FINE_PHI, axis=1)
    around = patch_rows % FINE_PHI
    lowest = jnp.min(around, axis=1)
    wrapped = jnp.max(around, axis=1) - lowest >= SIDE
    late = jnp.min(jnp.where(around >= FINE_PHI // 2, around, FINE_PHI), axis=1)
    return polar * ROW + jnp.where(wrapped, late, lowest)


def on_device(
    positions, forces, owner_map, near_target, near_source, near_patch, patch_rows, zone_rows
):
    devices = lax.axis_size(("blk", "tgt"))
    entries = near_target.shape[0]
    patches = patch_rows.shape[0]
    own = jnp.pad(jnp.concatenate([positions, forces], axis=0), ((0, 2), (0, WIDE - NODES)))
    inner = lax.axis_size("tgt")
    smem = pl.BlockSpec(memory_space=pltpu.SMEM)
    vmem = pl.BlockSpec(memory_space=pltpu.VMEM)
    node_shape = jax.ShapeDtypeStruct((3, NODES), jnp.float32)
    return pl.pallas_call(
        functools.partial(interactions, entries, patches, devices, inner),
        out_shape=(node_shape, node_shape),
        in_specs=[smem] * 4 + [vmem] * 3,
        out_specs=(vmem, vmem),
        scratch_shapes=[
            pltpu.VMEM((devices, 8, WIDE), jnp.float32),
            pltpu.VMEM((6, WIDE, LANES), jnp.float32),
            pltpu.VMEM((6, FINE_THETA * ROW, LANES), jnp.float32),
            pltpu.VMEM((WIDE, patches * LANES), jnp.bfloat16),
            pltpu.VMEM((patches, 3 * devices, LANES), jnp.float32),
            pltpu.VMEM((3, entries, LANES), jnp.float32),
            pltpu.VMEM((devices, 8, WIDE), jnp.float32),
            pltpu.VMEM((devices, 8, WIDE), jnp.float32),
            pltpu.VMEM((devices // 2, 8, LANES), jnp.float32),
            pltpu.VMEM((3, NODES, LANES), jnp.float32),
        ] + [pltpu.SemaphoreType.DMA((devices,))] * 4,
        compiler_params=pltpu.CompilerParams(
            collective_id=0, has_side_effects=True, vmem_limit_bytes=50 * 1024 * 1024
        ),
    )(near_target, owner_map, near_patch, patch_starts(patch_rows),
      jnp.stack([near_target, near_patch]), zone_rows, own)


def solution(mesh):
    nodes = P(None, ("groups", "blk", "tgt"))
    pairs = P(("groups", "blk", "tgt"))
    in_specs = (nodes, nodes, P("groups"), pairs, pairs, pairs, P(), P())
    return jax.shard_map(
        on_device, mesh=mesh, in_specs=in_specs, out_specs=(nodes, nodes), check_vma=False
    )
```

```python
import functools
import math

import jax
import jax.numpy as jnp
import numpy as np
from jax import lax
from jax.experimental import pallas as pl
from jax.experimental.pallas import tpu as pltpu
from jax.sharding import PartitionSpec as P

THETA = 13
PHI = 24
FINE_THETA = 37
FINE_PHI = 72
NODES = 312
FINE = 2664
LANES = 128
WIDE = 384
SIDE = 16
ROW = FINE_PHI + SIDE

FAR_BLOB = 0.09
NEAR_BLOB = 0.0025
STOKES_FACTOR = 1.0 / (8.0 * math.pi)
ENTRIES_STEP = 4
MESH = pl.DeviceIdType.MESH


def polar_taps():
    taps = []
    for fine_row in range(FINE_THETA):
        numerator = (2 * fine_row + 1) * THETA - FINE_THETA
        denominator = 2 * FINE_THETA
        lower_node = min(max(numerator // denominator, 0), THETA - 2)
        fraction = min(max((numerator - lower_node * denominator) / denominator, 0.0), 1.0)
        taps.append((lower_node, np.float32(1.0 - fraction), np.float32(fraction)))
    return taps


def pair_terms(x, y, f, sums):
    d = [x[k] - y[k] for k in range(3)]
    squared = d[0] * d[0] + d[1] * d[1] + (d[2] * d[2] + 1.0)
    inverse = lax.rsqrt(squared)
    cube = inverse * inverse * inverse
    direct = inverse + cube
    outer = (d[0] * f[0] + d[1] * f[1] + d[2] * f[2]) * cube
    return [sums[k] + (direct * f[k] + outer * d[k]) for k in range(3)]


def split3(value):
    high = value.astype(jnp.bfloat16)
    rest = value - high.astype(jnp.float32)
    middle = rest.astype(jnp.bfloat16)
    low = (rest - middle.astype(jnp.float32)).astype(jnp.bfloat16)
    return jnp.concatenate([high, middle, low], axis=0)


def zone_tables(patches, zone_ref, hot):
    nodes = lax.broadcasted_iota(jnp.int32, (WIDE, LANES), 0)
    for p in range(patches):
        found = nodes == zone_ref[p : p + 1, :]
        hot[:, p * LANES : (p + 1) * LANES] = jnp.where(found, 1.0, 0.0).astype(jnp.bfloat16)


def upsample(column, coarse, fine):
    for k in range(6):
        scale = np.float32(1.0 / math.sqrt(NEAR_BLOB)) if k < 3 else np.float32(1.0)
        coarse[k] = jnp.broadcast_to(column[:, k : k + 1] * scale, (WIDE, LANES))
    taps = polar_taps()

    def one_component(k, carry):
        for row, (lower, low_weight, high_weight) in enumerate(taps):
            here = coarse[k, pl.ds(lower * PHI, PHI), :] * low_weight
            here = here + coarse[k, pl.ds((lower + 1) * PHI, PHI), :] * high_weight
            after = jnp.concatenate([here[1:], here[:1]], axis=0)
            third = np.float32(1.0 / 3.0)
            step = (after - here) * third
            fine[k, pl.ds(row * ROW, PHI, stride=3), :] = here
            fine[k, pl.ds(row * ROW + 1, PHI, stride=3), :] = here + step
            fine[k, pl.ds(row * ROW + 2, PHI, stride=3), :] = after - step
            fine[k, pl.ds(row * ROW + FINE_PHI, SIDE), :] = fine[k, pl.ds(row * ROW, SIDE), :]
        return carry

    lax.fori_loop(0, 6, one_component, 0)


def near_part(entries, patches, devices, target_ref, owner_ref, patch_ref, start_ref,
              listed_ref, blocks, fine, hot, table, results, partial):
    spots = jnp.concatenate([blocks[:, k, :] for k in range(3)], axis=0)
    spots = split3(spots * np.float32(1.0 / math.sqrt(NEAR_BLOB)))
    count = 3 * devices
    batch = 8

    for first in range(0, patches, batch):
        picked = jnp.dot(
            spots, hot[:, first * LANES : (first + batch) * LANES],
            preferred_element_type=jnp.float32,
        )
        picked = (picked[2 * count :] + picked[count : 2 * count]) + picked[:count]
        for i in range(batch):
            table[first + i] = picked[:, i * LANES : (i + 1) * LANES]

    def some_entries(step, carry):
        for i in range(ENTRIES_STEP):
            e = step * ENTRIES_STEP + i
            target = owner_ref[target_ref[e]]
            p = patch_ref[e]
            base = start_ref[p, 0]
            x = [
                jnp.broadcast_to(table[p, pl.ds(k * devices + target, 1), :], (8, LANES))
                for k in range(3)
            ]
            sums = [jnp.zeros((8, LANES), jnp.float32)] * 3
            for row in range(SIDE):
                for half in range(2):
                    at = pl.ds(base + row * ROW + half * 8, 8)
                    y = [fine[k, at, :] for k in range(3)]
                    f = [fine[k + 3, at, :] for k in range(3)]
                    sums = pair_terms(x, y, f, sums)
            for k in range(3):
                results[k, pl.ds(e, 1), :] = jnp.sum(sums[k], axis=0, keepdims=True)
        return carry

    lax.fori_loop(0, entries // ENTRIES_STEP, some_entries, 0)

    named, region = listed_ref[0][...], listed_ref[1][...]
    slot = lax.fori_loop(
        0, devices, lambda v, found: jnp.where(named == v, owner_ref[v], found),
        jnp.zeros((1, entries), jnp.int32),
    )
    slots = lax.broadcasted_iota(jnp.int32, (devices, entries), 0)
    here = slots == slot
    values = split3(jnp.concatenate([results[k] for k in range(3)], axis=1))
    total = [jnp.zeros((3 * devices, WIDE), jnp.float32) for _ in range(3)]
    for first in range(0, patches, batch):
        chosen = jnp.concatenate(
            [jnp.where(here & (region == first + i), 1.0, 0.0) for i in range(batch)], axis=0
        ).astype(jnp.bfloat16)
        landed = jnp.dot(
            jnp.concatenate([chosen] * 3, axis=1), values, preferred_element_type=jnp.float32
        )
        for k in range(3):
            mine = landed[:, k * LANES : (k + 1) * LANES]
            mine = jnp.concatenate(
                [mine[i * devices : (i + 1) * devices] for i in range(batch)], axis=1
            )
            total[k] = total[k] + lax.dot_general(
                split3(mine), hot[:, first * LANES : (first + batch) * LANES],
                (((1,), (1,)), ((), ())), preferred_element_type=jnp.float32,
            )
    for k in range(3):
        moved = (total[k][2 * devices :] + total[k][devices : 2 * devices]) + total[k][:devices]
        partial[:, k, :] = moved * np.float32(STOKES_FACTOR * NODES / FINE / math.sqrt(NEAR_BLOB))


def far_part(devices, own_ref, blocks, coarse, tails, sums_ref, velocity):
    lane = lax.broadcasted_iota(jnp.int32, (8, LANES), 1)
    row = lax.broadcasted_iota(jnp.int32, (8, WIDE), 0)
    scale = jnp.where(row < 3, np.float32(1.0 / math.sqrt(FAR_BLOB)), np.float32(1.0))
    column = (own_ref[...] * scale).T
    for k in range(3):
        coarse[k] = jnp.broadcast_to(column[:, k : k + 1], (WIDE, LANES))

    def shrink(b, carry):
        blocks[b] = blocks[b] * scale
        return carry

    lax.fori_loop(0, devices, shrink, 0)

    def merge(b, carry):
        first = blocks[2 * b, :, pl.ds(2 * LANES, LANES)]
        second = blocks[2 * b + 1, :, pl.ds(2 * LANES, LANES)]
        tails[b] = jnp.where(lane < 64, first, pltpu.roll(second, 64, 1))
        return carry

    lax.fori_loop(0, devices // 2, merge, 0)
    group = 3

    def targets(g, carry):
        starts = [pl.multiple_of(g * (8 * group) + 8 * i, 8) for i in range(group)]
        x = [[coarse[k, pl.ds(s, 8), :] for k in range(3)] for s in starts]

        def sources(b, flat):
            sums = [list(flat[3 * i : 3 * i + 3]) for i in range(group)]
            rows = [
                lambda k, i=i, j=j: blocks[2 * b + i, pl.ds(k, 1), pl.ds(j * LANES, LANES)]
                for i in range(2)
                for j in range(2)
            ] + [lambda k: tails[b, pl.ds(k, 1), :]]
            for read in rows:
                values = [jnp.broadcast_to(read(k), (8, LANES)) for k in range(6)]
                for i in range(group):
                    sums[i] = pair_terms(x[i], values[:3], values[3:], sums[i])
            return tuple(v for s in sums for v in s)

        flat = tuple(jnp.zeros((8, LANES), jnp.float32) for _ in range(3 * group))
        flat = lax.fori_loop(0, devices // 2, sources, flat, unroll=4)
        for i in range(group):
            for k in range(3):
                sums_ref[k, pl.ds(starts[i], 8), :] = flat[3 * i + k]
        return carry

    lax.fori_loop(0, NODES // (8 * group), targets, 0)
    ones = jnp.ones((8, LANES), jnp.float32)
    for k in range(3):
        total = lax.dot_general(
            ones, sums_ref[k], (((1,), (1,)), ((), ())),
            precision=lax.Precision.HIGHEST, preferred_element_type=jnp.float32,
        )
        velocity[k : k + 1, :] = total[:1] * np.float32(STOKES_FACTOR / math.sqrt(FAR_BLOB))


def greet(me, devices, inner):
    barrier = pltpu.get_barrier_semaphore()

    def signal(i, carry):
        pl.semaphore_signal(
            barrier, inc=1, device_id=address(me, i, devices, inner), device_id_type=MESH
        )
        return carry

    lax.fori_loop(1, devices, signal, 0)
    pl.semaphore_wait(barrier, devices - 1)


def address(me, step, devices, inner):
    peer = lax.rem(me + step, devices)
    return {"blk": peer // inner, "tgt": lax.rem(peer, inner)}


def interactions(entries, patches, devices, inner, target_ref, owner_ref, patch_ref,
                 named_ref, region_ref, rows_ref, zone_ref, position_ref, force_ref,
                 velocity, patch_velocity, own_ref, start_vmem, start_ref, start_sem, blocks, coarse, fine, hot,
                 table, results, partial, landing, tails, sums_ref, sent, arrived, returned, landed):
    me = lax.axis_index("blk") * inner + lax.axis_index("tgt")

    def spread(step, slot):
        return pltpu.make_async_remote_copy(
            src_ref=own_ref, dst_ref=blocks.at[slot], send_sem=sent.at[step],
            recv_sem=arrived.at[slot], device_id=address(me, step, devices, inner),
            device_id_type=MESH,
        )

    def give_back(step, slot):
        return pltpu.make_async_remote_copy(
            src_ref=partial.at[lax.rem(me + step, devices)], dst_ref=landing.at[slot],
            send_sem=returned.at[step], recv_sem=landed.at[slot],
            device_id=address(me, step, devices, inner), device_id_type=MESH,
        )

    own_ref[...] = jnp.zeros((8, WIDE), jnp.float32)
    own_ref[0:3, 0:NODES] = position_ref[...]
    own_ref[3:6, 0:NODES] = force_ref[...]
    greet(me, devices, inner)

    def start(step, carry):
        spread(step, me).start()
        return carry

    lax.fori_loop(1, devices, start, 0)
    blocks[me] = own_ref[...]
    start_vmem[...] = jnp.broadcast_to(patch_starts(rows_ref[...]), (patches, LANES))
    starts = pltpu.make_async_copy(start_vmem, start_ref, start_sem)
    starts.start()
    upsample(own_ref[...].T, coarse, fine)
    zone_tables(patches, zone_ref, hot)
    starts.wait()

    def arrive(step, carry):
        spread(step, lax.rem(me + devices - step, devices)).wait()
        return carry

    lax.fori_loop(1, devices, arrive, 0)
    near_part(entries, patches, devices, target_ref, owner_ref, patch_ref, start_ref,
              (named_ref, region_ref), blocks, fine, hot, table, results, partial)

    def start_back(step, carry):
        give_back(step, me).start()
        return carry

    lax.fori_loop(1, devices, start_back, 0)
    far_part(devices, own_ref, blocks, coarse, tails, sums_ref, velocity)

    def finish(step, total):
        slot = lax.rem(me + devices - step, devices)
        give_back(step, slot).wait()
        return total + landing[slot]

    total = lax.fori_loop(1, devices, finish, partial[me])
    patch_velocity[...] = total[:3, :NODES]


def patch_starts(rows):
    row = lax.shift_right_logical(rows * 14564, 20)
    around = rows - row * FINE_PHI
    lowest = jnp.min(around, axis=1, keepdims=True)
    wrapped = jnp.max(around, axis=1, keepdims=True) - lowest >= SIDE
    late = jnp.min(jnp.where(around >= FINE_PHI // 2, around, FINE_PHI), axis=1, keepdims=True)
    return jnp.min(row, axis=1, keepdims=True) * ROW + jnp.where(wrapped, late, lowest)


def on_device(
    positions, forces, owner_map, near_target, near_source, near_patch, patch_rows, zone_rows
):
    devices = lax.axis_size(("blk", "tgt"))
    entries = near_target.shape[0]
    patches = patch_rows.shape[0]
    inner = lax.axis_size("tgt")
    smem = pl.BlockSpec(memory_space=pltpu.SMEM)
    vmem = pl.BlockSpec(memory_space=pltpu.VMEM)
    node_shape = jax.ShapeDtypeStruct((3, NODES), jnp.float32)
    return pl.pallas_call(
        functools.partial(interactions, entries, patches, devices, inner),
        out_shape=(node_shape, node_shape),
        in_specs=[smem] * 3 + [vmem] * 6,
        out_specs=(vmem, vmem),
        scratch_shapes=[
            pltpu.VMEM((8, WIDE), jnp.float32),
            pltpu.VMEM((patches, LANES), jnp.int32),
            pltpu.SMEM((patches, LANES), jnp.int32),
            pltpu.SemaphoreType.DMA,
            pltpu.VMEM((devices, 8, WIDE), jnp.float32),
            pltpu.VMEM((6, WIDE, LANES), jnp.float32),
            pltpu.VMEM((6, FINE_THETA * ROW, LANES), jnp.float32),
            pltpu.VMEM((WIDE, patches * LANES), jnp.bfloat16),
            pltpu.VMEM((patches, 3 * devices, LANES), jnp.float32),
            pltpu.VMEM((3, entries, LANES), jnp.float32),
            pltpu.VMEM((devices, 8, WIDE), jnp.float32),
            pltpu.VMEM((devices, 8, WIDE), jnp.float32),
            pltpu.VMEM((devices // 2, 8, LANES), jnp.float32),
            pltpu.VMEM((3, NODES, LANES), jnp.float32),
        ] + [pltpu.SemaphoreType.DMA((devices,))] * 4,
        compiler_params=pltpu.CompilerParams(
            collective_id=0, has_side_effects=True, vmem_limit_bytes=50 * 1024 * 1024
        ),
    )(near_target, owner_map, near_patch, near_target.reshape(1, entries),
      near_patch.reshape(1, entries), patch_rows, zone_rows, positions, forces)


def solution(mesh):
    nodes = P(None, ("groups", "blk", "tgt"))
    pairs = P(("groups", "blk", "tgt"))
    in_specs = (nodes, nodes, P("groups"), pairs, pairs, pairs, P(), P())
    return jax.shard_map(
        on_device, mesh=mesh, in_specs=in_specs, out_specs=(nodes, nodes), check_vma=False
    )
```

```python
import functools
import math

import jax
import jax.numpy as jnp
import numpy as np
from jax import lax
from jax.experimental import pallas as pl
from jax.experimental.pallas import tpu as pltpu
from jax.sharding import PartitionSpec as P

THETA = 13
PHI = 24
FINE_THETA = 37
FINE_PHI = 72
NODES = 312
FINE = 2664
LANES = 128
WIDE = 384
SIDE = 16
ROW = FINE_PHI + SIDE

FAR_BLOB = 0.09
NEAR_BLOB = 0.0025
STOKES_FACTOR = 1.0 / (8.0 * math.pi)
ENTRIES_STEP = 2
MESH = pl.DeviceIdType.MESH


def polar_taps():
    taps = []
    for fine_row in range(FINE_THETA):
        numerator = (2 * fine_row + 1) * THETA - FINE_THETA
        denominator = 2 * FINE_THETA
        lower_node = min(max(numerator // denominator, 0), THETA - 2)
        fraction = min(max((numerator - lower_node * denominator) / denominator, 0.0), 1.0)
        taps.append((lower_node, np.float32(1.0 - fraction), np.float32(fraction)))
    return taps


def pair_terms(x, y, f, sums):
    d = [x[k] - y[k] for k in range(3)]
    squared = d[0] * d[0] + d[1] * d[1] + (d[2] * d[2] + 1.0)
    inverse = lax.rsqrt(squared)
    cube = inverse * inverse * inverse
    direct = inverse + cube
    outer = (d[0] * f[0] + d[1] * f[1] + d[2] * f[2]) * cube
    return [sums[k] + (direct * f[k] + outer * d[k]) for k in range(3)]


def split3(value):
    high = value.astype(jnp.bfloat16)
    rest = value - high.astype(jnp.float32)
    middle = rest.astype(jnp.bfloat16)
    low = (rest - middle.astype(jnp.float32)).astype(jnp.bfloat16)
    return jnp.concatenate([high, middle, low], axis=0)


def zone_tables(patches, zone_ref, hot):
    nodes = lax.broadcasted_iota(jnp.int32, (WIDE, LANES), 0)
    for p in range(patches):
        found = nodes == zone_ref[p : p + 1, :]
        hot[:, p * LANES : (p + 1) * LANES] = jnp.where(found, 1.0, 0.0).astype(jnp.bfloat16)


def upsample(column, coarse, fine):
    for k in range(6):
        scale = np.float32(1.0 / math.sqrt(NEAR_BLOB)) if k < 3 else np.float32(1.0)
        coarse[k] = jnp.broadcast_to(column[:, k : k + 1] * scale, (WIDE, LANES))
    taps = polar_taps()

    def one_component(k, carry):
        for row, (lower, low_weight, high_weight) in enumerate(taps):
            here = coarse[k, pl.ds(lower * PHI, PHI), :] * low_weight
            here = here + coarse[k, pl.ds((lower + 1) * PHI, PHI), :] * high_weight
            after = jnp.concatenate([here[1:], here[:1]], axis=0)
            third = np.float32(1.0 / 3.0)
            step = (after - here) * third
            fine[k, pl.ds(row * ROW, PHI, stride=3), :] = here
            fine[k, pl.ds(row * ROW + 1, PHI, stride=3), :] = here + step
            fine[k, pl.ds(row * ROW + 2, PHI, stride=3), :] = after - step
            fine[k, pl.ds(row * ROW + FINE_PHI, SIDE), :] = fine[k, pl.ds(row * ROW, SIDE), :]
        return carry

    lax.fori_loop(0, 6, one_component, 0)


def near_part(entries, patches, devices, target_ref, owner_ref, patch_ref, start_ref,
              listed_ref, blocks, fine, hot, table, results, partial):
    spots = jnp.concatenate([blocks[:, k, :] for k in range(3)], axis=0)
    spots = split3(spots * np.float32(1.0 / math.sqrt(NEAR_BLOB)))
    count = 3 * devices
    batch = 8

    for first in range(0, patches, batch):
        picked = jnp.dot(
            spots, hot[:, first * LANES : (first + batch) * LANES],
            preferred_element_type=jnp.float32,
        )
        picked = (picked[2 * count :] + picked[count : 2 * count]) + picked[:count]
        for i in range(batch):
            table[first + i] = picked[:, i * LANES : (i + 1) * LANES]

    def some_entries(step, carry):
        for i in range(ENTRIES_STEP):
            e = step * ENTRIES_STEP + i
            target = owner_ref[target_ref[e]]
            p = patch_ref[e]
            base = start_ref[p, 0]
            x = [
                jnp.broadcast_to(table[p, pl.ds(k * devices + target, 1), :], (8, LANES))
                for k in range(3)
            ]
            sums = [jnp.zeros((8, LANES), jnp.float32)] * 3
            for row in range(SIDE):
                for half in range(2):
                    at = pl.ds(base + row * ROW + half * 8, 8)
                    y = [fine[k, at, :] for k in range(3)]
                    f = [fine[k + 3, at, :] for k in range(3)]
                    sums = pair_terms(x, y, f, sums)
            for k in range(3):
                results[k, pl.ds(e, 1), :] = jnp.sum(sums[k], axis=0, keepdims=True)
        return carry

    lax.fori_loop(0, entries // ENTRIES_STEP, some_entries, 0)

    named, region = listed_ref[0][...], listed_ref[1][...]
    slot = lax.fori_loop(
        0, devices, lambda v, found: jnp.where(named == v, owner_ref[v], found),
        jnp.zeros((1, entries), jnp.int32),
    )
    slots = lax.broadcasted_iota(jnp.int32, (devices, entries), 0)
    here = slots == slot
    values = split3(jnp.concatenate([results[k] for k in range(3)], axis=1))
    total = [jnp.zeros((3 * devices, WIDE), jnp.float32) for _ in range(3)]
    for first in range(0, patches, batch):
        chosen = jnp.concatenate(
            [jnp.where(here & (region == first + i), 1.0, 0.0) for i in range(batch)], axis=0
        ).astype(jnp.bfloat16)
        landed = jnp.dot(
            jnp.concatenate([chosen] * 3, axis=1), values, preferred_element_type=jnp.float32
        )
        for k in range(3):
            mine = landed[:, k * LANES : (k + 1) * LANES]
            mine = jnp.concatenate(
                [mine[i * devices : (i + 1) * devices] for i in range(batch)], axis=1
            )
            total[k] = total[k] + lax.dot_general(
                split3(mine), hot[:, first * LANES : (first + batch) * LANES],
                (((1,), (1,)), ((), ())), preferred_element_type=jnp.float32,
            )
    for k in range(3):
        moved = (total[k][2 * devices :] + total[k][devices : 2 * devices]) + total[k][:devices]
        partial[:, k, :] = moved * np.float32(STOKES_FACTOR * NODES / FINE / math.sqrt(NEAR_BLOB))


def far_part(devices, own_ref, blocks, coarse, tails, sums_ref, velocity):
    lane = lax.broadcasted_iota(jnp.int32, (8, LANES), 1)
    row = lax.broadcasted_iota(jnp.int32, (8, WIDE), 0)
    scale = jnp.where(row < 3, np.float32(1.0 / math.sqrt(FAR_BLOB)), np.float32(1.0))
    column = (own_ref[...] * scale).T
    for k in range(3):
        coarse[k] = jnp.broadcast_to(column[:, k : k + 1], (WIDE, LANES))

    def shrink(b, carry):
        blocks[b] = blocks[b] * scale
        return carry

    lax.fori_loop(0, devices, shrink, 0)

    def merge(b, carry):
        first = blocks[2 * b, :, pl.ds(2 * LANES, LANES)]
        second = blocks[2 * b + 1, :, pl.ds(2 * LANES, LANES)]
        tails[b] = jnp.where(lane < 64, first, pltpu.roll(second, 64, 1))
        return carry

    lax.fori_loop(0, devices // 2, merge, 0)
    group = 3

    def targets(g, carry):
        starts = [pl.multiple_of(g * (8 * group) + 8 * i, 8) for i in range(group)]
        x = [[coarse[k, pl.ds(s, 8), :] for k in range(3)] for s in starts]

        def sources(b, flat):
            sums = [list(flat[3 * i : 3 * i + 3]) for i in range(group)]
            rows = [
                lambda k, i=i, j=j: blocks[2 * b + i, pl.ds(k, 1), pl.ds(j * LANES, LANES)]
                for i in range(2)
                for j in range(2)
            ] + [lambda k: tails[b, pl.ds(k, 1), :]]
            for read in rows:
                values = [jnp.broadcast_to(read(k), (8, LANES)) for k in range(6)]
                for i in range(group):
                    sums[i] = pair_terms(x[i], values[:3], values[3:], sums[i])
            return tuple(v for s in sums for v in s)

        flat = tuple(jnp.zeros((8, LANES), jnp.float32) for _ in range(3 * group))
        flat = lax.fori_loop(0, devices // 2, sources, flat, unroll=2)
        for i in range(group):
            for k in range(3):
                sums_ref[k, pl.ds(starts[i], 8), :] = flat[3 * i + k]
        return carry

    lax.fori_loop(0, NODES // (8 * group), targets, 0)
    ones = jnp.ones((8, LANES), jnp.float32)
    for k in range(3):
        total = lax.dot_general(
            ones, sums_ref[k], (((1,), (1,)), ((), ())),
            precision=lax.Precision.HIGHEST, preferred_element_type=jnp.float32,
        )
        velocity[k : k + 1, :] = total[:1] * np.float32(STOKES_FACTOR / math.sqrt(FAR_BLOB))


def greet(me, devices, inner):
    barrier = pltpu.get_barrier_semaphore()

    def signal(i, carry):
        pl.semaphore_signal(
            barrier, inc=1, device_id=address(me, i, devices, inner), device_id_type=MESH
        )
        return carry

    lax.fori_loop(1, devices, signal, 0)
    pl.semaphore_wait(barrier, devices - 1)


def address(me, step, devices, inner):
    peer = lax.rem(me + step, devices)
    return {"blk": peer // inner, "tgt": lax.rem(peer, inner)}


def interactions(entries, patches, devices, inner, target_ref, owner_ref, patch_ref,
                 named_ref, region_ref, rows_hbm, zone_hbm, position_hbm, force_hbm,
                 velocity, patch_velocity, rows_ref, zone_ref, position_ref, force_ref, load_sem,
                 own_ref, start_vmem, start_ref, start_sem, blocks, coarse, fine, hot,
                 table, results, partial, landing, tails, sums_ref, sent, arrived, returned, landed):
    me = lax.axis_index("blk") * inner + lax.axis_index("tgt")

    def spread(step, slot):
        return pltpu.make_async_remote_copy(
            src_ref=own_ref, dst_ref=blocks.at[slot], send_sem=sent.at[step],
            recv_sem=arrived.at[slot], device_id=address(me, step, devices, inner),
            device_id_type=MESH,
        )

    def give_back(step, slot):
        return pltpu.make_async_remote_copy(
            src_ref=partial.at[lax.rem(me + step, devices)], dst_ref=landing.at[slot],
            send_sem=returned.at[step], recv_sem=landed.at[slot],
            device_id=address(me, step, devices, inner), device_id_type=MESH,
        )

    pairs = ((position_hbm, position_ref), (force_hbm, force_ref),
             (rows_hbm, rows_ref), (zone_hbm, zone_ref))
    loads = [pltpu.make_async_copy(*pair, load_sem.at[i]) for i, pair in enumerate(pairs)]
    for load in loads:
        load.start()
    greet(me, devices, inner)
    own_ref[...] = jnp.zeros((8, WIDE), jnp.float32)
    loads[0].wait()
    loads[1].wait()
    own_ref[0:3, 0:NODES] = position_ref[...]
    own_ref[3:6, 0:NODES] = force_ref[...]

    def start(step, carry):
        spread(step, me).start()
        return carry

    lax.fori_loop(1, devices, start, 0)
    blocks[me] = own_ref[...]
    loads[2].wait()
    loads[3].wait()
    start_vmem[...] = jnp.broadcast_to(patch_starts(rows_ref[...]), (patches, LANES))
    starts = pltpu.make_async_copy(start_vmem, start_ref, start_sem)
    starts.start()
    upsample(own_ref[...].T, coarse, fine)
    zone_tables(patches, zone_ref, hot)
    starts.wait()

    def arrive(step, carry):
        spread(step, lax.rem(me + devices - step, devices)).wait()
        return carry

    lax.fori_loop(1, devices, arrive, 0)
    near_part(entries, patches, devices, target_ref, owner_ref, patch_ref, start_ref,
              (named_ref, region_ref), blocks, fine, hot, table, results, partial)

    def start_back(step, carry):
        give_back(step, me).start()
        return carry

    lax.fori_loop(1, devices, start_back, 0)
    far_part(devices, own_ref, blocks, coarse, tails, sums_ref, velocity)

    def finish(step, total):
        slot = lax.rem(me + devices - step, devices)
        give_back(step, slot).wait()
        return total + landing[slot]

    total = lax.fori_loop(1, devices, finish, partial[me])
    patch_velocity[...] = total[:3, :NODES]


def patch_starts(rows):
    row = lax.shift_right_logical(rows * 14564, 20)
    around = rows - row * FINE_PHI
    lowest = jnp.min(around, axis=1, keepdims=True)
    wrapped = jnp.max(around, axis=1, keepdims=True) - lowest >= SIDE
    late = jnp.min(jnp.where(around >= FINE_PHI // 2, around, FINE_PHI), axis=1, keepdims=True)
    return jnp.min(row, axis=1, keepdims=True) * ROW + jnp.where(wrapped, late, lowest)


def on_device(
    positions, forces, owner_map, near_target, near_source, near_patch, patch_rows, zone_rows
):
    devices = lax.axis_size(("blk", "tgt"))
    entries = near_target.shape[0]
    patches = patch_rows.shape[0]
    inner = lax.axis_size("tgt")
    smem = pl.BlockSpec(memory_space=pltpu.SMEM)
    vmem = pl.BlockSpec(memory_space=pltpu.VMEM)
    node_shape = jax.ShapeDtypeStruct((3, NODES), jnp.float32)
    return pl.pallas_call(
        functools.partial(interactions, entries, patches, devices, inner),
        out_shape=(node_shape, node_shape),
        in_specs=[smem] * 3 + [vmem] * 2 + [pl.BlockSpec(memory_space=pl.ANY)] * 4,
        out_specs=(vmem, vmem),
        scratch_shapes=[
            pltpu.VMEM(patch_rows.shape, jnp.int32),
            pltpu.VMEM(zone_rows.shape, jnp.int32),
            pltpu.VMEM(positions.shape, jnp.float32),
            pltpu.VMEM(forces.shape, jnp.float32),
            pltpu.SemaphoreType.DMA((4,)),
            pltpu.VMEM((8, WIDE), jnp.float32),
            pltpu.VMEM((patches, LANES), jnp.int32),
            pltpu.SMEM((patches, LANES), jnp.int32),
            pltpu.SemaphoreType.DMA,
            pltpu.VMEM((devices, 8, WIDE), jnp.float32),
            pltpu.VMEM((6, WIDE, LANES), jnp.float32),
            pltpu.VMEM((6, FINE_THETA * ROW, LANES), jnp.float32),
            pltpu.VMEM((WIDE, patches * LANES), jnp.bfloat16),
            pltpu.VMEM((patches, 3 * devices, LANES), jnp.float32),
            pltpu.VMEM((3, entries, LANES), jnp.float32),
            pltpu.VMEM((devices, 8, WIDE), jnp.float32),
            pltpu.VMEM((devices, 8, WIDE), jnp.float32),
            pltpu.VMEM((devices // 2, 8, LANES), jnp.float32),
            pltpu.VMEM((3, NODES, LANES), jnp.float32),
        ] + [pltpu.SemaphoreType.DMA((devices,))] * 4,
        compiler_params=pltpu.CompilerParams(
            collective_id=0, has_side_effects=True, vmem_limit_bytes=50 * 1024 * 1024
        ),
    )(near_target, owner_map, near_patch, near_target.reshape(1, entries),
      near_patch.reshape(1, entries), patch_rows, zone_rows, positions, forces)


def solution(mesh):
    nodes = P(None, ("groups", "blk", "tgt"))
    pairs = P(("groups", "blk", "tgt"))
    in_specs = (nodes, nodes, P("groups"), pairs, pairs, pairs, P(), P())
    return jax.shard_map(
        on_device, mesh=mesh, in_specs=in_specs, out_specs=(nodes, nodes), check_vma=False
    )
```
